128 devices in a mesh: frame: 4 (over y_hi, core), tok: 16 (over x, z), dp: 2 (over y_lo).
Axes of the slice: x: 4, y: 4 (y_hi: 2, y_lo: 2; y = y_hi * 2 + y_lo), z: 4, core: 2. Of those that a mesh axis runs over, the one named last changes fastest.
Arguments:
- queries: bfloat16 [4, 1024, 2048], P('dp', 'tok', 'frame'), may hold values from -200 to 200
- bank: bfloat16 [4, 8, 1024, 4096], P('dp', 'frame', 'tok'), may hold values from -4 to 4
- read_mask: int32 [4, 8], P('dp', 'frame'), may hold values from 0 to 1, as said below
Outputs:
- attended: bfloat16 [4, 1024, 2048], P('dp', 'tok', 'frame')
The draws below stay inside these ranges and needn't reach their ends.
Inputs may be any that keep to these rules, and one draw needn't show every extreme that they name: `read_mask`: each sample reads between 4 and 8 frames, always its frame 0; in every draw some sample reads all 8 frames and some reads exactly 4.
All inputs are finite; a program needn't handle non-finite values.
Results may differ from the reference program's by a relative error of at most 0.0049.
Values may be sent and summed in bfloat16 or wider, within the bound.
A program may use at most 128 MiB of HBM per device.

```python
import math
import jax
import jax.numpy as jnp
from jax import lax

HEADS = 32
HEAD_DIM = 64
NTOK = 1024
SAMPLES = 4
FRAMES = 8


def shared_lead(key):
    return jnp.clip(jax.random.normal(key, (SAMPLES, NTOK, HEADS * HEAD_DIM), jnp.float32), -4.0, 4.0)


def draw_bank(key, part):
    lead = shared_lead(key)
    key = jax.random.fold_in(key, 11)
    width = HEADS * HEAD_DIM
    base = jnp.clip(jax.random.normal(key, (SAMPLES, FRAMES, NTOK, 2 * width), jnp.float32), -4.0, 4.0)
    base = base.at[:, 0, :, :width].set(lead)
    return base.astype(jnp.bfloat16)


def draw_queries(key, part):
    key = jax.random.fold_in(key, 12)
    shape = (SAMPLES, NTOK, HEADS * HEAD_DIM)
    result = 0.5 * jnp.clip(jax.random.normal(key, shape, jnp.float32), -4.0, 4.0)
    return result.astype(jnp.bfloat16)


def draw_read_mask(key, part):
    key = jax.random.fold_in(key, 13)
    count_key, order_key = jax.random.split(key)
    counts = jax.random.randint(count_key, (SAMPLES,), 4, FRAMES + 1)
    sample_ids = jnp.arange(SAMPLES)
    counts = jnp.where(sample_ids == 0, FRAMES, jnp.where(sample_ids == SAMPLES - 1, 4, counts))
    orders = jax.vmap(lambda single: jax.random.permutation(single, FRAMES - 1))(jax.random.split(order_key, SAMPLES))
    rest = (orders < (counts - 1)[:, None]).astype(jnp.int32)
    first = jnp.ones((SAMPLES, 1), jnp.int32)
    return jnp.concatenate([first, rest], axis=1)


def setup_inputs(seed: int = 0) -> dict:
    arg_keys = jax.random.split(jax.random.key(seed), 4)
    queries = draw_queries(jax.random.fold_in(arg_keys[3], 71), 0)
    bank = draw_bank(jax.random.fold_in(arg_keys[3], 71), 0)
    read_mask = draw_read_mask(jax.random.fold_in(arg_keys[3], 71), 0)
    return {"queries": queries, "bank": bank, "read_mask": read_mask}


NEG_FILL = -1e+30

def reference(queries, bank, read_mask):
    scale = 1.0 / math.sqrt(HEAD_DIM)
    width = HEADS * HEAD_DIM

    def one_sample(items):
        query_rows, frames, chosen = items
        query_rows = query_rows.astype(jnp.float32).reshape(NTOK, HEADS, HEAD_DIM)

        def frame_scores(frame_rows):
            keys_f = frame_rows[:, :width].astype(jnp.float32).reshape(NTOK, HEADS, HEAD_DIM)
            return jnp.einsum('qhd,khd->qhk', query_rows, keys_f) * scale

        def peak_step(peak, item):
            frame_rows, flag = item
            scores = jnp.where(flag == 1, frame_scores(frame_rows), jnp.float32(NEG_FILL))
            return (jnp.maximum(peak, scores.max(-1)), None)
        start = jnp.full((NTOK, HEADS), NEG_FILL, jnp.float32)
        peak, _ = lax.scan(peak_step, start, (frames, chosen))

        def sum_step(carry, item):
            numer, denom = carry
            frame_rows, flag = item
            scores = frame_scores(frame_rows)
            probs = jnp.where(flag == 1, jnp.exp(scores - peak[:, :, None]), jnp.float32(0.0))
            denom = denom + probs.sum(-1)
            rounded = lax.optimization_barrier(probs.astype(jnp.bfloat16))
            values_f = frame_rows[:, width:].astype(jnp.float32).reshape(NTOK, HEADS, HEAD_DIM)
            numer = numer + jnp.einsum('qhk,khd->qhd', rounded.astype(jnp.float32), values_f)
            return ((numer, denom), None)
        zero_numer = jnp.zeros((NTOK, HEADS, HEAD_DIM), jnp.float32)
        zero_denom = jnp.zeros((NTOK, HEADS), jnp.float32)
        (numer, denom), _ = lax.scan(sum_step, (zero_numer, zero_denom), (frames, chosen))
        return (numer / denom[:, :, None]).reshape(NTOK, width).astype(jnp.bfloat16)
    return lax.map(one_sample, (queries, bank, read_mask))
```

```python
import math

import jax
import jax.numpy as jnp
from jax import lax
from jax.experimental import pallas as pl
from jax.experimental.pallas import tpu as pltpu
from jax.sharding import PartitionSpec as P

MESH = pl.DeviceIdType.MESH
HEAD_DIM = 64
PAIR = 2 * HEAD_DIM
TOK = 64
KEYS_COLS = 2048
MASKED = -1e30
FLOOR = -1e20

ORDER = (0, 29, 18, 12, 11, 27, 2, 6, 31, 8, 17, 10, 20, 30, 14, 22, 1, 21, 24, 7, 13, 23, 15, 16, 4, 9, 3, 25, 26, 28, 19, 5)
GROUP = 4
GROUPS = 32 // GROUP


def kernel(q_ref, bank_ref, mask_ref, out_ref, q_buf, q_heads, kv, bias, mask_tile, acc, peak, outs,
           q_send, q_recv, kv_send, kv_recv, fwd_send, fwd_recv, mask_send, mask_recv, out_send, out_recv):
    frame, tok = lax.axis_index("frame"), lax.axis_index("tok")
    y, core = frame // 2, frame % 2
    x, z = tok // 4, tok % 4
    samp, pair = tok // 8, tok % 8

    barrier = pltpu.get_barrier_semaphore()
    for i in range(1, 64):
        pl.semaphore_signal(
            barrier, inc=1, device_id={"frame": (frame + i // 16) % 4, "tok": (tok + i % 16) % 16}, device_id_type=MESH
        )
    mask_tile[...] = jnp.zeros_like(mask_tile)
    for s in range(2):
        for j in range(2):
            flag = (mask_ref[s, j].astype(jnp.float32) - 1.0) * (-MASKED)
            mask_tile[pl.ds(2 * s + j, 1), :] = jnp.full((1, 128), flag, jnp.float32)
    bias[pl.ds(frame, 1)] = mask_tile[...][None]
    pl.semaphore_wait(barrier, 63)

    def send_or_keep(src, dst, send_sem, recv_sem, to_frame, to_tok):
        here = (to_frame == frame) & (to_tok == tok)

        @pl.when(here)
        def _():
            pltpu.make_async_copy(src, dst, recv_sem).start()

        @pl.when(jnp.logical_not(here))
        def _():
            pltpu.make_async_remote_copy(
                src, dst, send_sem, recv_sem, device_id={"frame": to_frame, "tok": to_tok}, device_id_type=MESH
            ).start()

    def wait_sent(blocks, sem):
        kept = (tok // 8 == core) & (pair // 4 == core)

        @pl.when(kept)
        def _():
            pltpu.make_async_copy(blocks.at[pl.ds(0, 7)], blocks.at[pl.ds(0, 7)], sem).wait()

        @pl.when(jnp.logical_not(kept))
        def _():
            pltpu.make_async_copy(blocks, blocks, sem).wait()

    for i in range(1, 4):
        pltpu.make_async_remote_copy(
            mask_tile, bias.at[frame], mask_send, mask_recv, device_id={"frame": (frame + i) % 4}, device_id_type=MESH
        ).start()
    for s in range(2):
        for j in range(4):
            send_or_keep(
                q_ref.at[s, :, pl.ds(j * PAIR, PAIR)], q_buf.at[tok % 8], q_send, q_recv,
                2 * y + tok // 8, 8 * s + 4 * core + j,
            )
    for slot, code in enumerate(ORDER):
        dy, dx, dz = code // 16, code // 4 % 4, code % 4
        dx = jnp.where(core == 1, (4 - dx) % 4, dx)
        dz = jnp.where(core == 1, (4 - dz) % 4, dz)
        to_y, to_tok = (y + dy) % 2, (x + dx) % 4 * 4 + (z + dz) % 4
        column = (8 * to_y + to_tok % 8) * PAIR
        for part in range(2):
            src = bank_ref.at[to_tok // 8, :, :, pl.ds(pl.multiple_of(part * KEYS_COLS + column, PAIR), PAIR)]
            dst = kv.at[0, slot, part]
            if code == 0:
                pltpu.make_async_copy(src, dst, kv_recv.at[slot // GROUP]).start()
            else:
                pltpu.make_async_remote_copy(
                    src, dst, kv_send, kv_recv.at[slot // GROUP],
                    device_id={"frame": 2 * to_y + core, "tok": to_tok}, device_id_type=MESH,
                ).start()

    acc[...] = jnp.zeros_like(acc)
    peak[...] = jnp.full_like(peak, FLOOR)
    others = bias.at[pl.ds(0, 3)]
    pltpu.make_async_copy(others, others, mask_recv).wait()
    pltpu.make_async_copy(q_buf, q_buf, q_recv).wait()
    queries = q_buf[...].reshape(8 * TOK, PAIR).astype(jnp.float32) * (1.0 / math.sqrt(HEAD_DIM))
    first = lax.broadcasted_iota(jnp.int32, queries.shape, 1) < HEAD_DIM
    q_heads[0] = jnp.where(first, queries, 0.0).astype(jnp.bfloat16)
    q_heads[1] = jnp.where(first, 0.0, queries).astype(jnp.bfloat16)

    def work(half, group, from_core):
        keys = kv[half, pl.ds(group * GROUP, GROUP), 0].reshape(GROUP * 2 * TOK, PAIR)
        values = kv[half, pl.ds(group * GROUP, GROUP), 1].reshape(GROUP * 2 * TOK, PAIR)
        values_t = values.T
        top = lax.broadcasted_iota(jnp.int32, values_t.shape, 0) < HEAD_DIM
        one = jnp.ones_like(values_t)
        biases = []
        for i in range(GROUP):
            dy = ORDER_DY[group * GROUP + i]
            from_frame = 2 * ((y + dy) % 2) + from_core
            for j in range(2):
                row = bias[pl.ds(from_frame, 1), pl.ds(2 * samp + j, 1), :].reshape(1, 128)
                biases.append(jnp.concatenate([row] * 4, axis=1))
        for head in range(2):
            scores = lax.dot_general(
                keys, q_heads[head], (((1,), (1,)), ((), ())), preferred_element_type=jnp.float32
            ).reshape(GROUP * 2, TOK, 8 * TOK)
            tops = [scores[i].max(axis=0, keepdims=True) + biases[i] for i in range(GROUP * 2)]
            old = peak[head]
            new = old
            for t in tops:
                new = jnp.maximum(new, t)
            peak[head] = new
            probs = jnp.concatenate(
                [jnp.exp(scores[i] - (new - biases[i])).astype(jnp.bfloat16) for i in range(GROUP * 2)], axis=0
            )
            weighed = jnp.where(top, values_t, one) if head == 0 else jnp.where(top, one, values_t)
            acc[head] = acc[head] * jnp.exp(old - new) + jnp.dot(weighed, probs, preferred_element_type=jnp.float32)

    for group in range(GROUPS):
        mine = kv.at[0, pl.ds(group * GROUP, GROUP)]
        pltpu.make_async_copy(mine, mine, kv_recv.at[group]).wait()
        forward = pltpu.make_async_remote_copy(
            mine, kv.at[1, pl.ds(group * GROUP, GROUP)], fwd_send, fwd_recv.at[group],
            device_id={"frame": 2 * y + 1 - core}, device_id_type=MESH,
        )
        forward.start()
        work(0, group, core)
        forward.wait_recv()
        work(1, group, 1 - core)

    result = jnp.concatenate(
        [acc[0, :HEAD_DIM] / acc[0, HEAD_DIM:], acc[1, HEAD_DIM:] / acc[1, :HEAD_DIM]], axis=0
    )
    outs[...] = result.T.astype(jnp.bfloat16).reshape(8, TOK, PAIR)
    owner_frame = 2 * y + pair // 4
    for i in range(8):
        column = pl.multiple_of(pair % 4 * PAIR, PAIR)
        send_or_keep(
            outs.at[i], out_ref.at[samp, :, pl.ds(column, PAIR)], out_send, out_recv, owner_frame, 8 * core + i
        )

    pltpu.make_async_copy(out_ref, out_ref, out_recv).wait()
    wait_sent(outs, out_send)
    wait_sent(q_buf, q_send)
    pltpu.make_async_copy(others, others, mask_send).wait()
    sent = kv.at[0, pl.ds(0, 31)]
    pltpu.make_async_copy(sent, sent, kv_send).wait()
    pltpu.make_async_copy(kv.at[0], kv.at[0], fwd_send).wait()


ORDER_DY = [code // 16 for code in ORDER]


def body(queries, bank, read_mask):
    return pl.pallas_call(
        kernel,
        out_shape=jax.ShapeDtypeStruct(queries.shape, queries.dtype),
        in_specs=[
            pl.BlockSpec(memory_space=pl.ANY),
            pl.BlockSpec(memory_space=pl.ANY),
            pl.BlockSpec(memory_space=pltpu.SMEM),
        ],
        out_specs=pl.BlockSpec(memory_space=pl.ANY),
        scratch_shapes=[
            pltpu.VMEM((8, TOK, PAIR), jnp.bfloat16),
            pltpu.VMEM((2, 8 * TOK, PAIR), jnp.bfloat16),
            pltpu.VMEM((2, 32, 2, 2, TOK, PAIR), jnp.bfloat16),
            pltpu.VMEM((4, 8, 128), jnp.float32),
            pltpu.VMEM((8, 128), jnp.float32),
            pltpu.VMEM((2, PAIR, 8 * TOK), jnp.float32),
            pltpu.VMEM((2, 1, 8 * TOK), jnp.float32),
            pltpu.VMEM((8, TOK, PAIR), jnp.bfloat16),
            pltpu.SemaphoreType.DMA,
            pltpu.SemaphoreType.DMA,
            pltpu.SemaphoreType.DMA,
            pltpu.SemaphoreType.DMA((GROUPS,)),
            pltpu.SemaphoreType.DMA,
            pltpu.SemaphoreType.DMA((GROUPS,)),
            pltpu.SemaphoreType.DMA,
            pltpu.SemaphoreType.DMA,
            pltpu.SemaphoreType.DMA,
            pltpu.SemaphoreType.DMA,
        ],
        compiler_params=pltpu.CompilerParams(
            collective_id=0, has_side_effects=True, vmem_limit_bytes=48 * 1024 * 1024
        ),
    )(queries, bank, read_mask)


def solution(mesh):
    return jax.shard_map(
        body,
        mesh=mesh,
        in_specs=(P("dp", "tok", "frame"), P("dp", "frame", "tok", None), P("dp", "frame")),
        out_specs=P("dp", "tok", "frame"),
        check_vma=False,
    )
```

```python
import math

import jax
import jax.numpy as jnp
from jax import lax
from jax.experimental import pallas as pl
from jax.experimental.pallas import tpu as pltpu
from jax.sharding import PartitionSpec as P

MESH = pl.DeviceIdType.MESH
HEAD_DIM = 64
PAIR = 2 * HEAD_DIM
TOK = 64
KEYS_COLS = 2048
MASKED = -1e30
FLOOR = -1e20

ORDER = (0, 4, 12, 1, 3, 16, 5, 7, 13, 15, 20, 2, 28, 17, 8, 19, 6, 9, 21, 23, 29, 11, 14, 31, 18, 24, 10, 22, 25, 27, 30, 26)
SIZES = (4, 4, 4, 4, 4, 4, 4, 4)
STARTS = tuple(sum(SIZES[:i]) for i in range(len(SIZES)))
GROUPS = len(SIZES)
BATCHES = (6,) + (2,) * 13
BATCH_STARTS = tuple(sum(BATCHES[:i]) for i in range(len(BATCHES)))
GROUP_OF = tuple(i for i, size in enumerate(SIZES) for _ in range(size))
NEAR = 4
FLY = 8


def kernel(q_ref, bank_ref, mask_ref, out_ref, q_buf, q_heads, kv, bias, mask_tile, mask_smem, acc, peak, outs,
           q_send, q_recv, kv_send, kv_recv, fwd_send, fwd_recv, mask_send, mask_recv, mask_copy,
           out_send, out_recv, plane_sem, sibling_sem, far_sem):
    frame, tok = lax.axis_index("frame"), lax.axis_index("tok")
    y, core = frame // 2, frame % 2
    x, z = tok // 4, tok % 4
    samp, pair = tok // 8, tok % 8
    sibling = 2 * y + 1 - core
    across = (frame + 2) % 4
    x_mates = [((x + i) % 4) * 4 + z for i in range(1, 4)]
    z_mates = [x * 4 + (z + i) % 4 for i in range(1, 4)]

    def tell(sem, to_frame, to_tok):
        pl.semaphore_signal(sem, inc=1, device_id={"frame": to_frame, "tok": to_tok}, device_id_type=MESH)

    def send(src, dst, send_sem, recv_sem, to_frame, to_tok):
        copy = pltpu.make_async_remote_copy(
            src, dst, send_sem, recv_sem, device_id={"frame": to_frame, "tok": to_tok}, device_id_type=MESH
        )
        copy.start()

    def send_or_keep(src, dst, send_sem, recv_sem, to_frame, to_tok):
        here = (to_frame == frame) & (to_tok == tok)

        @pl.when(here)
        def _():
            pltpu.make_async_copy(src, dst, recv_sem).start()

        @pl.when(jnp.logical_not(here))
        def _():
            send(src, dst, send_sem, recv_sem, to_frame, to_tok)

    def wait_bytes(ref, sem):
        pltpu.make_async_copy(ref, ref, sem).wait()

    def wait_sent(blocks, sem, kept):
        @pl.when(kept)
        def _():
            wait_bytes(blocks.at[pl.ds(0, 7)], sem)

        @pl.when(jnp.logical_not(kept))
        def _():
            wait_bytes(blocks, sem)

    def send_batch(batch):
        for slot in range(BATCH_STARTS[batch], BATCH_STARTS[batch] + BATCHES[batch]):
            code = ORDER[slot]
            dy, dx, dz = code // 16, code // 4 % 4, code % 4
            dx = jnp.where(core == 1, (4 - dx) % 4, dx)
            dz = jnp.where(core == 1, (4 - dz) % 4, dz)
            to_y, to_tok = (y + dy) % 2, (x + dx) % 4 * 4 + (z + dz) % 4
            column = (8 * to_y + to_tok % 8) * PAIR
            arrived = kv_recv.at[GROUP_OF[slot]]
            for part in range(2):
                src = bank_ref.at[to_tok // 8, :, :, pl.ds(pl.multiple_of(part * KEYS_COLS + column, PAIR), PAIR)]
                dst = kv.at[0, slot, part]
                if code == 0:
                    pltpu.make_async_copy(src, dst, arrived).start()
                else:
                    send(src, dst, kv_send.at[batch], arrived, 2 * to_y + core, to_tok)

    def wait_batch_sent(batch):
        sent = BATCHES[batch] - (1 if batch == 0 else 0)
        wait_bytes(kv.at[0, pl.ds(0, sent)], kv_send.at[batch])

    def send_next(batch):
        if batch < len(BATCHES):
            wait_batch_sent(batch - FLY)
            send_batch(batch)

    barrier = pltpu.get_barrier_semaphore()
    tell(barrier, sibling, tok)
    tell(barrier, across, tok)
    for mate in x_mates + z_mates:
        tell(barrier, frame, mate)
    pltpu.make_async_copy(mask_ref, mask_smem, mask_copy).start()
    mask_tile[...] = jnp.zeros_like(mask_tile)
    acc[...] = jnp.zeros_like(acc)
    peak[...] = jnp.full_like(peak, FLOOR)
    wait_bytes(mask_smem, mask_copy)
    for s in range(2):
        for j in range(2):
            flag = (mask_smem[s, j].astype(jnp.float32) - 1.0) * (-MASKED)
            mask_tile[pl.ds(2 * s + j, 1), :] = jnp.full((1, 128), flag, jnp.float32)
    bias[pl.ds(frame, 1)] = mask_tile[...][None]
    pl.semaphore_wait(barrier, 8)

    for mate in x_mates:
        tell(plane_sem, frame, mate)
    send_batch(0)
    pl.semaphore_wait(plane_sem, 3)

    tell(sibling_sem, sibling, tok)
    tell(far_sem, across, tok)
    pl.semaphore_wait(sibling_sem, 1)
    for s in range(2):
        for j in range(4):
            send_or_keep(
                q_ref.at[s, :, pl.ds(j * PAIR, PAIR)], q_buf.at[tok % 8], q_send, q_recv,
                2 * y + tok // 8, 8 * s + 4 * core + j,
            )
    for batch in range(1, NEAR):
        send_batch(batch)
    pl.semaphore_wait(far_sem, 1)
    for batch in range(NEAR, FLY):
        send_batch(batch)
    for i in range(1, 4):
        send(mask_tile, bias.at[frame], mask_send, mask_recv, (frame + i) % 4, tok)
    send_next(FLY)
    wait_bytes(q_buf, q_recv)
    others = bias.at[pl.ds(0, 3)]
    wait_bytes(others, mask_recv)

    queries = q_buf[...].reshape(8 * TOK, PAIR).astype(jnp.float32) * (1.0 / math.sqrt(HEAD_DIM))
    first = lax.broadcasted_iota(jnp.int32, queries.shape, 1) < HEAD_DIM
    q_heads[0] = jnp.where(first, queries, 0.0).astype(jnp.bfloat16)
    q_heads[1] = jnp.where(first, 0.0, queries).astype(jnp.bfloat16)

    def work(half, group, from_core):
        start, size = STARTS[group], SIZES[group]
        keys = kv[half, pl.ds(start, size), 0].reshape(size * 2 * TOK, PAIR)
        values = kv[half, pl.ds(start, size), 1].reshape(size * 2 * TOK, PAIR)
        values_t = values.T
        top = lax.broadcasted_iota(jnp.int32, values_t.shape, 0) < HEAD_DIM
        one = jnp.ones_like(values_t)
        biases = []
        for i in range(size):
            dy = ORDER[start + i] // 16
            from_frame = 2 * ((y + dy) % 2) + from_core
            for j in range(2):
                row = bias[pl.ds(from_frame, 1), pl.ds(2 * samp + j, 1), :].reshape(1, 128)
                biases.append(jnp.concatenate([row] * 4, axis=1))
        both = [
            lax.dot_general(
                keys, q_heads[head], (((1,), (1,)), ((), ())), preferred_element_type=jnp.float32
            ).reshape(size * 2, TOK, 8 * TOK)
            for head in range(2)
        ]
        for head, scores in enumerate(both):
            old = peak[head]
            new = old
            for i in range(size * 2):
                new = jnp.maximum(new, scores[i].max(axis=0, keepdims=True) + biases[i])
            peak[head] = new
            probs = jnp.concatenate(
                [jnp.exp(scores[i] - (new - biases[i])).astype(jnp.bfloat16) for i in range(size * 2)], axis=0
            )
            weighed = jnp.where(top, values_t, one) if head == 0 else jnp.where(top, one, values_t)
            acc[head] = acc[head] * jnp.exp(old - new) + jnp.dot(weighed, probs, preferred_element_type=jnp.float32)

    for group in range(GROUPS):
        mine = kv.at[0, pl.ds(STARTS[group], SIZES[group])]
        theirs = kv.at[1, pl.ds(STARTS[group], SIZES[group])]
        send_next(FLY + 1 + 2 * group)
        wait_bytes(mine, kv_recv.at[group])
        send(mine, theirs, fwd_send, fwd_recv.at[group], sibling, tok)
        work(0, group, core)
        send_next(FLY + 2 + 2 * group)
        wait_bytes(theirs, fwd_recv.at[group])
        work(1, group, 1 - core)

    result = jnp.concatenate(
        [acc[0, :HEAD_DIM] / acc[0, HEAD_DIM:], acc[1, HEAD_DIM:] / acc[1, :HEAD_DIM]], axis=0
    )
    outs[...] = result.T.astype(jnp.bfloat16).reshape(8, TOK, PAIR)
    owner_frame = 2 * y + pair // 4
    for i in range(8):
        column = pl.multiple_of(pair % 4 * PAIR, PAIR)
        send_or_keep(
            outs.at[i], out_ref.at[samp, :, pl.ds(column, PAIR)], out_send, out_recv, owner_frame, 8 * core + i
        )

    wait_bytes(out_ref, out_recv)
    kept = (tok // 8 == core) & (pair // 4 == core)
    wait_sent(outs, out_send, kept)
    wait_sent(q_buf, q_send, kept)
    wait_bytes(others, mask_send)
    for batch in range(len(BATCHES) - FLY, len(BATCHES)):
        wait_batch_sent(batch)
    wait_bytes(kv.at[0], fwd_send)


def body(queries, bank, read_mask):
    return pl.pallas_call(
        kernel,
        out_shape=jax.ShapeDtypeStruct(queries.shape, queries.dtype),
        in_specs=[
            pl.BlockSpec(memory_space=pltpu.HBM),
            pl.BlockSpec(memory_space=pltpu.HBM),
            pl.BlockSpec(memory_space=pltpu.HBM),
        ],
        out_specs=pl.BlockSpec(memory_space=pl.ANY),
        scratch_shapes=[
            pltpu.VMEM((8, TOK, PAIR), jnp.bfloat16),
            pltpu.VMEM((2, 8 * TOK, PAIR), jnp.bfloat16),
            pltpu.VMEM((2, 32, 2, 2, TOK, PAIR), jnp.bfloat16),
            pltpu.VMEM((4, 8, 128), jnp.float32),
            pltpu.VMEM((8, 128), jnp.float32),
            pltpu.SMEM((2, 2), jnp.int32),
            pltpu.VMEM((2, PAIR, 8 * TOK), jnp.float32),
            pltpu.VMEM((2, 1, 8 * TOK), jnp.float32),
            pltpu.VMEM((8, TOK, PAIR), jnp.bfloat16),
            pltpu.SemaphoreType.DMA,
            pltpu.SemaphoreType.DMA,
            pltpu.SemaphoreType.DMA((len(BATCHES),)),
            pltpu.SemaphoreType.DMA((GROUPS,)),
            pltpu.SemaphoreType.DMA,
            pltpu.SemaphoreType.DMA((GROUPS,)),
            pltpu.SemaphoreType.DMA,
            pltpu.SemaphoreType.DMA,
            pltpu.SemaphoreType.DMA,
            pltpu.SemaphoreType.DMA,
            pltpu.SemaphoreType.DMA,
            pltpu.SemaphoreType.REGULAR,
            pltpu.SemaphoreType.REGULAR,
            pltpu.SemaphoreType.REGULAR,
        ],
        compiler_params=pltpu.CompilerParams(
            collective_id=0, has_side_effects=True, vmem_limit_bytes=48 * 1024 * 1024
        ),
    )(queries, bank, read_mask)


def solution(mesh):
    return jax.shard_map(
        body,
        mesh=mesh,
        in_specs=(P("dp", "tok", "frame"), P("dp", "frame", "tok", None), P("dp", "frame")),
        out_specs=P("dp", "tok", "frame"),
        check_vma=False,
    )
```

```python
import math

import jax
import jax.numpy as jnp
from jax import lax
from jax.experimental import pallas as pl
from jax.experimental.pallas import tpu as pltpu
from jax.sharding import PartitionSpec as P

MESH = pl.DeviceIdType.MESH
HEAD_DIM = 64
PAIR = 2 * HEAD_DIM
TOK = 64
KEYS_COLS = 2048
MASKED = -1e30
FLOOR = -1e20

ORDER = (0, 4, 12, 1, 3, 16, 20, 5, 28, 15, 24, 2, 8, 7, 13, 6, 9, 11, 17, 19, 21, 31, 23, 29, 18, 14, 25, 27, 22, 30, 10, 26)
SIZES = (4, 4, 4, 4, 4, 4, 4, 4)
STARTS = tuple(sum(SIZES[:i]) for i in range(len(SIZES)))
GROUPS = len(SIZES)
BATCHES = (6,) + (2,) * 13
BATCH_STARTS = tuple(sum(BATCHES[:i]) for i in range(len(BATCHES)))
GROUP_OF = tuple(i for i, size in enumerate(SIZES) for _ in range(size))
NEAR = 7
FLY = 10


def kernel(q_ref, bank_ref, mask_ref, out_ref, q_buf, q_heads, kv, bias, mask_tile, mask_smem, acc, peak, outs,
           q_send, q_recv, kv_send, kv_recv, fwd_send, fwd_recv, mask_send, mask_recv, mask_copy,
           out_send, out_recv, plane_sem, sibling_sem, far_sem):
    frame, tok = lax.axis_index("frame"), lax.axis_index("tok")
    y, core = frame // 2, frame % 2
    x, z = tok // 4, tok % 4
    samp, pair = tok // 8, tok % 8
    sibling = 2 * y + 1 - core
    across = (frame + 2) % 4
    x_mates = [((x + i) % 4) * 4 + z for i in range(1, 4)]
    z_mates = [x * 4 + (z + i) % 4 for i in range(1, 4)]

    def tell(sem, to_frame, to_tok):
        pl.semaphore_signal(sem, inc=1, device_id={"frame": to_frame, "tok": to_tok}, device_id_type=MESH)

    def send(src, dst, send_sem, recv_sem, to_frame, to_tok):
        copy = pltpu.make_async_remote_copy(
            src, dst, send_sem, recv_sem, device_id={"frame": to_frame, "tok": to_tok}, device_id_type=MESH
        )
        copy.start()

    def send_or_keep(src, dst, send_sem, recv_sem, to_frame, to_tok):
        here = (to_frame == frame) & (to_tok == tok)

        @pl.when(here)
        def _():
            pltpu.make_async_copy(src, dst, recv_sem).start()

        @pl.when(jnp.logical_not(here))
        def _():
            send(src, dst, send_sem, recv_sem, to_frame, to_tok)

    def wait_bytes(ref, sem):
        pltpu.make_async_copy(ref, ref, sem).wait()

    def wait_sent(blocks, sem, kept):
        @pl.when(kept)
        def _():
            wait_bytes(blocks.at[pl.ds(0, 7)], sem)

        @pl.when(jnp.logical_not(kept))
        def _():
            wait_bytes(blocks, sem)

    def send_batch(batch):
        for slot in range(BATCH_STARTS[batch], BATCH_STARTS[batch] + BATCHES[batch]):
            code = ORDER[slot]
            dy, dx, dz = code // 16, code // 4 % 4, code % 4
            dx = jnp.where(core == 1, (4 - dx) % 4, dx)
            dz = jnp.where(core == 1, (4 - dz) % 4, dz)
            to_y, to_tok = (y + dy) % 2, (x + dx) % 4 * 4 + (z + dz) % 4
            column = (8 * to_y + to_tok % 8) * PAIR
            arrived = kv_recv.at[GROUP_OF[slot]]
            for part in range(2):
                src = bank_ref.at[to_tok // 8, :, :, pl.ds(pl.multiple_of(part * KEYS_COLS + column, PAIR), PAIR)]
                dst = kv.at[0, slot, part]
                if code == 0:
                    pltpu.make_async_copy(src, dst, arrived).start()
                else:
                    send(src, dst, kv_send.at[batch], arrived, 2 * to_y + core, to_tok)

    def wait_batch_sent(batch):
        sent = BATCHES[batch] - (1 if batch == 0 else 0)
        wait_bytes(kv.at[0, pl.ds(0, sent)], kv_send.at[batch])

    def send_next(batch):
        if batch < len(BATCHES):
            wait_batch_sent(batch - FLY)
            send_batch(batch)

    barrier = pltpu.get_barrier_semaphore()
    tell(barrier, sibling, tok)
    tell(barrier, across, tok)
    for mate in x_mates + z_mates:
        tell(barrier, frame, mate)
    pltpu.make_async_copy(mask_ref, mask_smem, mask_copy).start()
    mask_tile[...] = jnp.zeros_like(mask_tile)
    acc[...] = jnp.zeros_like(acc)
    peak[...] = jnp.full_like(peak, FLOOR)
    wait_bytes(mask_smem, mask_copy)
    for s in range(2):
        for j in range(2):
            flag = (mask_smem[s, j].astype(jnp.float32) - 1.0) * (-MASKED)
            mask_tile[pl.ds(2 * s + j, 1), :] = jnp.full((1, 128), flag, jnp.float32)
    bias[pl.ds(frame, 1)] = mask_tile[...][None]
    pl.semaphore_wait(barrier, 8)

    for mate in x_mates:
        tell(plane_sem, frame, mate)
    send_batch(0)
    pl.semaphore_wait(plane_sem, 3)

    tell(sibling_sem, sibling, tok)
    tell(far_sem, across, tok)
    pl.semaphore_wait(sibling_sem, 1)
    for s in range(2):
        for j in range(4):
            send_or_keep(
                q_ref.at[s, :, pl.ds(j * PAIR, PAIR)], q_buf.at[tok % 8], q_send, q_recv,
                2 * y + tok // 8, 8 * s + 4 * core + j,
            )
    for batch in range(1, NEAR):
        send_batch(batch)
    pl.semaphore_wait(far_sem, 1)
    for batch in range(NEAR, FLY):
        send_batch(batch)
    for i in range(1, 4):
        send(mask_tile, bias.at[frame], mask_send, mask_recv, (frame + i) % 4, tok)
    send_next(FLY)
    wait_bytes(q_buf, q_recv)
    others = bias.at[pl.ds(0, 3)]
    wait_bytes(others, mask_recv)

    queries = q_buf[...].reshape(8 * TOK, PAIR).astype(jnp.float32) * (1.0 / math.sqrt(HEAD_DIM))
    first = lax.broadcasted_iota(jnp.int32, queries.shape, 1) < HEAD_DIM
    q_heads[0] = jnp.where(first, queries, 0.0).astype(jnp.bfloat16)
    q_heads[1] = jnp.where(first, 0.0, queries).astype(jnp.bfloat16)

    def work(half, group, from_core):
        start, size = STARTS[group], SIZES[group]
        keys = kv[half, pl.ds(start, size), 0].reshape(size * 2 * TOK, PAIR)
        values = kv[half, pl.ds(start, size), 1].reshape(size * 2 * TOK, PAIR)
        values_t = values.T
        top = lax.broadcasted_iota(jnp.int32, values_t.shape, 0) < HEAD_DIM
        one = jnp.ones_like(values_t)
        biases = []
        for i in range(size):
            dy = ORDER[start + i] // 16
            from_frame = 2 * ((y + dy) % 2) + from_core
            for j in range(2):
                row = bias[pl.ds(from_frame, 1), pl.ds(2 * samp + j, 1), :].reshape(1, 128)
                biases.append(jnp.concatenate([row] * 4, axis=1))
        both = [
            lax.dot_general(
                keys, q_heads[head], (((1,), (1,)), ((), ())), preferred_element_type=jnp.float32
            ).reshape(size * 2, TOK, 8 * TOK)
            for head in range(2)
        ]
        for head, scores in enumerate(both):
            old = peak[head]
            new = old
            for i in range(size * 2):
                new = jnp.maximum(new, scores[i].max(axis=0, keepdims=True) + biases[i])
            peak[head] = new
            probs = jnp.concatenate(
                [jnp.exp(scores[i] - (new - biases[i])).astype(jnp.bfloat16) for i in range(size * 2)], axis=0
            )
            weighed = jnp.where(top, values_t, one) if head == 0 else jnp.where(top, one, values_t)
            acc[head] = acc[head] * jnp.exp(old - new) + jnp.dot(weighed, probs, preferred_element_type=jnp.float32)

    for group in range(GROUPS):
        mine = kv.at[0, pl.ds(STARTS[group], SIZES[group])]
        theirs = kv.at[1, pl.ds(STARTS[group], SIZES[group])]
        send_next(FLY + 1 + 2 * group)
        wait_bytes(mine, kv_recv.at[group])
        send(mine, theirs, fwd_send, fwd_recv.at[group], sibling, tok)
        work(0, group, core)
        send_next(FLY + 2 + 2 * group)
        wait_bytes(theirs, fwd_recv.at[group])
        work(1, group, 1 - core)

    result = jnp.concatenate(
        [acc[0, :HEAD_DIM] / acc[0, HEAD_DIM:], acc[1, HEAD_DIM:] / acc[1, :HEAD_DIM]], axis=0
    )
    outs[...] = result.T.astype(jnp.bfloat16).reshape(8, TOK, PAIR)
    owner_frame = 2 * y + pair // 4
    for i in range(8):
        column = pl.multiple_of(pair % 4 * PAIR, PAIR)
        send_or_keep(
            outs.at[i], out_ref.at[samp, :, pl.ds(column, PAIR)], out_send, out_recv, owner_frame, 8 * core + i
        )

    wait_bytes(out_ref, out_recv)
    kept = (tok // 8 == core) & (pair // 4 == core)
    wait_sent(outs, out_send, kept)
    wait_sent(q_buf, q_send, kept)
    wait_bytes(others, mask_send)
    for batch in range(len(BATCHES) - FLY, len(BATCHES)):
        wait_batch_sent(batch)
    wait_bytes(kv.at[0], fwd_send)


def body(queries, bank, read_mask):
    return pl.pallas_call(
        kernel,
        out_shape=jax.ShapeDtypeStruct(queries.shape, queries.dtype),
        in_specs=[
            pl.BlockSpec(memory_space=pltpu.HBM),
            pl.BlockSpec(memory_space=pltpu.HBM),
            pl.BlockSpec(memory_space=pltpu.HBM),
        ],
        out_specs=pl.BlockSpec(memory_space=pl.ANY),
        scratch_shapes=[
            pltpu.VMEM((8, TOK, PAIR), jnp.bfloat16),
            pltpu.VMEM((2, 8 * TOK, PAIR), jnp.bfloat16),
            pltpu.VMEM((2, 32, 2, 2, TOK, PAIR), jnp.bfloat16),
            pltpu.VMEM((4, 8, 128), jnp.float32),
            pltpu.VMEM((8, 128), jnp.float32),
            pltpu.SMEM((2, 2), jnp.int32),
            pltpu.VMEM((2, PAIR, 8 * TOK), jnp.float32),
            pltpu.VMEM((2, 1, 8 * TOK), jnp.float32),
            pltpu.VMEM((8, TOK, PAIR), jnp.bfloat16),
            pltpu.SemaphoreType.DMA,
            pltpu.SemaphoreType.DMA,
            pltpu.SemaphoreType.DMA((len(BATCHES),)),
            pltpu.SemaphoreType.DMA((GROUPS,)),
            pltpu.SemaphoreType.DMA,
            pltpu.SemaphoreType.DMA((GROUPS,)),
            pltpu.SemaphoreType.DMA,
            pltpu.SemaphoreType.DMA,
            pltpu.SemaphoreType.DMA,
            pltpu.SemaphoreType.DMA,
            pltpu.SemaphoreType.DMA,
            pltpu.SemaphoreType.REGULAR,
            pltpu.SemaphoreType.REGULAR,
            pltpu.SemaphoreType.REGULAR,
        ],
        compiler_params=pltpu.CompilerParams(
            collective_id=0, has_side_effects=True, vmem_limit_bytes=48 * 1024 * 1024
        ),
    )(queries, bank, read_mask)


def solution(mesh):
    return jax.shard_map(
        body,
        mesh=mesh,
        in_specs=(P("dp", "tok", "frame"), P("dp", "frame", "tok", None), P("dp", "frame")),
        out_specs=P("dp", "tok", "frame"),
        check_vma=False,
    )
```

```python
import math

import jax
import jax.numpy as jnp
from jax import lax
from jax.experimental import pallas as pl
from jax.experimental.pallas import tpu as pltpu
from jax.sharding import PartitionSpec as P

MESH = pl.DeviceIdType.MESH
HEAD_DIM = 64
PAIR = 2 * HEAD_DIM
TOK = 64
KEYS_COLS = 2048
MASKED = -1e30
FLOOR = -1e20

ORDER = (0, 4, 12, 1, 3, 16, 20, 5, 28, 15, 24, 2, 8, 7, 13, 6, 9, 11, 17, 19, 21, 31, 23, 29, 18, 14, 25, 27, 22, 30, 10, 26)
SIZES = (4, 4, 4, 4, 4, 4, 4, 4)
STARTS = tuple(sum(SIZES[:i]) for i in range(len(SIZES)))
GROUPS = len(SIZES)
BATCHES = (6,) + (2,) * 13
BATCH_STARTS = tuple(sum(BATCHES[:i]) for i in range(len(BATCHES)))
GROUP_OF = tuple(i for i, size in enumerate(SIZES) for _ in range(size))
NEAR = 7
FLY = 10


def kernel(q_ref, bank_ref, mask_ref, out_ref, q_buf, q_heads, kv, bias, mask_tile, mask_smem, acc, peak, outs,
           q_send, q_recv, kv_send, kv_recv, fwd_send, fwd_recv, mask_send, mask_recv, mask_copy,
           out_send, out_recv, plane_sem, sibling_sem, far_sem):
    frame, tok = lax.axis_index("frame"), lax.axis_index("tok")
    y, core = frame // 2, frame % 2
    x, z = tok // 4, tok % 4
    samp, pair = tok // 8, tok % 8
    sibling = 2 * y + 1 - core
    across = (frame + 2) % 4
    x_mates = [((x + i) % 4) * 4 + z for i in range(1, 4)]
    z_mates = [x * 4 + (z + i) % 4 for i in range(1, 4)]

    def tell(sem, to_frame, to_tok):
        pl.semaphore_signal(sem, inc=1, device_id={"frame": to_frame, "tok": to_tok}, device_id_type=MESH)

    def send(src, dst, send_sem, recv_sem, to_frame, to_tok):
        copy = pltpu.make_async_remote_copy(
            src, dst, send_sem, recv_sem, device_id={"frame": to_frame, "tok": to_tok}, device_id_type=MESH
        )
        copy.start()

    def send_or_keep(src, dst, send_sem, recv_sem, to_frame, to_tok):
        here = (to_frame == frame) & (to_tok == tok)

        @pl.when(here)
        def _():
            pltpu.make_async_copy(src, dst, recv_sem).start()

        @pl.when(jnp.logical_not(here))
        def _():
            send(src, dst, send_sem, recv_sem, to_frame, to_tok)

    def wait_bytes(ref, sem):
        pltpu.make_async_copy(ref, ref, sem).wait()

    def wait_sent(blocks, sem, kept):
        @pl.when(kept)
        def _():
            wait_bytes(blocks.at[pl.ds(0, 7)], sem)

        @pl.when(jnp.logical_not(kept))
        def _():
            wait_bytes(blocks, sem)

    def send_batch(batch):
        for slot in range(BATCH_STARTS[batch], BATCH_STARTS[batch] + BATCHES[batch]):
            code = ORDER[slot]
            dy, dx, dz = code // 16, code // 4 % 4, code % 4
            dx = jnp.where(core == 1, (4 - dx) % 4, dx)
            dz = jnp.where(core == 1, (4 - dz) % 4, dz)
            to_y, to_tok = (y + dy) % 2, (x + dx) % 4 * 4 + (z + dz) % 4
            column = (8 * to_y + to_tok % 8) * PAIR
            arrived = kv_recv.at[GROUP_OF[slot]]
            for part in range(2):
                src = bank_ref.at[to_tok // 8, :, :, pl.ds(pl.multiple_of(part * KEYS_COLS + column, PAIR), PAIR)]
                dst = kv.at[0, slot, part]
                if code == 0:
                    pltpu.make_async_copy(src, dst, arrived).start()
                else:
                    send(src, dst, kv_send.at[batch], arrived, 2 * to_y + core, to_tok)

    def wait_batch_sent(batch):
        sent = BATCHES[batch] - (1 if batch == 0 else 0)
        wait_bytes(kv.at[0, pl.ds(0, sent)], kv_send.at[batch])

    def send_next(batch):
        if batch < len(BATCHES):
            wait_batch_sent(batch - FLY)
            send_batch(batch)

    barrier = pltpu.get_barrier_semaphore()
    tell(barrier, sibling, tok)
    tell(barrier, across, tok)
    for mate in x_mates + z_mates:
        tell(barrier, frame, mate)
    pltpu.make_async_copy(mask_ref, mask_smem, mask_copy).start()
    mask_tile[...] = jnp.zeros_like(mask_tile)
    acc[...] = jnp.zeros_like(acc)
    peak[...] = jnp.full_like(peak, FLOOR)
    wait_bytes(mask_smem, mask_copy)
    for s in range(2):
        for j in range(2):
            flag = (mask_smem[s, j].astype(jnp.float32) - 1.0) * (-MASKED)
            mask_tile[pl.ds(2 * s + j, 1), :] = jnp.full((1, 128), flag, jnp.float32)
    bias[pl.ds(frame, 1)] = mask_tile[...][None]
    pl.semaphore_wait(barrier, 8)

    for mate in x_mates:
        tell(plane_sem, frame, mate)
    mine_mask, far_mask = bias.at[frame], bias.at[across]
    send(mask_tile, mine_mask, mask_send.at[0], mask_recv.at[0], across, tok)
    send(mask_tile, mine_mask, mask_send.at[1], mask_recv.at[1], sibling, tok)
    send_batch(0)
    pl.semaphore_wait(plane_sem, 3)

    tell(sibling_sem, sibling, tok)
    tell(far_sem, across, tok)
    pl.semaphore_wait(sibling_sem, 1)
    for s in range(2):
        for j in range(4):
            send_or_keep(
                q_ref.at[s, :, pl.ds(j * PAIR, PAIR)], q_buf.at[tok % 8], q_send, q_recv,
                2 * y + tok // 8, 8 * s + 4 * core + j,
            )
    wait_bytes(far_mask, mask_recv.at[0])
    send(far_mask, far_mask, mask_send.at[2], mask_recv.at[2], sibling, tok)
    for batch in range(1, NEAR):
        send_batch(batch)
    pl.semaphore_wait(far_sem, 1)
    for batch in range(NEAR, FLY):
        send_batch(batch)
    send_next(FLY)
    wait_bytes(q_buf, q_recv)
    wait_bytes(mine_mask, mask_recv.at[1])
    wait_bytes(mine_mask, mask_recv.at[2])
    queries = q_buf[...].reshape(8 * TOK, PAIR).astype(jnp.float32) * (1.0 / math.sqrt(HEAD_DIM))
    first = lax.broadcasted_iota(jnp.int32, queries.shape, 1) < HEAD_DIM
    q_heads[0] = jnp.where(first, queries, 0.0).astype(jnp.bfloat16)
    q_heads[1] = jnp.where(first, 0.0, queries).astype(jnp.bfloat16)

    def work(half, group, from_core):
        start, size = STARTS[group], SIZES[group]
        keys = kv[half, pl.ds(start, size), 0].reshape(size * 2 * TOK, PAIR)
        values = kv[half, pl.ds(start, size), 1].reshape(size * 2 * TOK, PAIR)
        values_t = values.T
        top = lax.broadcasted_iota(jnp.int32, values_t.shape, 0) < HEAD_DIM
        one = jnp.ones_like(values_t)
        biases = []
        for i in range(size):
            dy = ORDER[start + i] // 16
            from_frame = 2 * ((y + dy) % 2) + from_core
            for j in range(2):
                row = bias[pl.ds(from_frame, 1), pl.ds(2 * samp + j, 1), :].reshape(1, 128)
                biases.append(jnp.concatenate([row] * 4, axis=1))
        both = [
            lax.dot_general(
                keys, q_heads[head], (((1,), (1,)), ((), ())), preferred_element_type=jnp.float32
            ).reshape(size * 2, TOK, 8 * TOK)
            for head in range(2)
        ]
        for head, scores in enumerate(both):
            old = peak[head]
            new = old
            for i in range(size * 2):
                new = jnp.maximum(new, scores[i].max(axis=0, keepdims=True) + biases[i])
            peak[head] = new
            probs = jnp.concatenate(
                [jnp.exp(scores[i] - (new - biases[i])).astype(jnp.bfloat16) for i in range(size * 2)], axis=0
            )
            weighed = jnp.where(top, values_t, one) if head == 0 else jnp.where(top, one, values_t)
            acc[head] = acc[head] * jnp.exp(old - new) + jnp.dot(weighed, probs, preferred_element_type=jnp.float32)

    for group in range(GROUPS):
        mine = kv.at[0, pl.ds(STARTS[group], SIZES[group])]
        theirs = kv.at[1, pl.ds(STARTS[group], SIZES[group])]
        send_next(FLY + 1 + 2 * group)
        wait_bytes(mine, kv_recv.at[group])
        send(mine, theirs, fwd_send, fwd_recv.at[group], sibling, tok)
        work(0, group, core)
        send_next(FLY + 2 + 2 * group)
        wait_bytes(theirs, fwd_recv.at[group])
        work(1, group, 1 - core)

    owner_frame = 2 * y + pair // 4
    column = pl.multiple_of(pair % 4 * PAIR, PAIR)
    for part in range(2):
        cols = pl.ds(part * 4 * TOK, 4 * TOK)
        result = jnp.concatenate(
            [
                acc[0, pl.ds(0, HEAD_DIM), cols] / acc[0, pl.ds(HEAD_DIM, HEAD_DIM), cols],
                acc[1, pl.ds(HEAD_DIM, HEAD_DIM), cols] / acc[1, pl.ds(0, HEAD_DIM), cols],
            ],
            axis=0,
        )
        outs[pl.ds(4 * part, 4)] = result.T.astype(jnp.bfloat16).reshape(4, TOK, PAIR)
        for i in range(4 * part, 4 * part + 4):
            send_or_keep(
                outs.at[i], out_ref.at[samp, :, pl.ds(column, PAIR)], out_send, out_recv, owner_frame, 8 * core + i
            )

    wait_bytes(out_ref, out_recv)
    kept = (tok // 8 == core) & (pair // 4 == core)
    wait_sent(outs, out_send, kept)
    wait_sent(q_buf, q_send, kept)
    for i in range(3):
        wait_bytes(mask_tile, mask_send.at[i])
    for batch in range(len(BATCHES) - FLY, len(BATCHES)):
        wait_batch_sent(batch)
    wait_bytes(kv.at[0], fwd_send)


def body(queries, bank, read_mask):
    return pl.pallas_call(
        kernel,
        out_shape=jax.ShapeDtypeStruct(queries.shape, queries.dtype),
        in_specs=[
            pl.BlockSpec(memory_space=pltpu.HBM),
            pl.BlockSpec(memory_space=pltpu.HBM),
            pl.BlockSpec(memory_space=pltpu.HBM),
        ],
        out_specs=pl.BlockSpec(memory_space=pl.ANY),
        scratch_shapes=[
            pltpu.VMEM((8, TOK, PAIR), jnp.bfloat16),
            pltpu.VMEM((2, 8 * TOK, PAIR), jnp.bfloat16),
            pltpu.VMEM((2, 32, 2, 2, TOK, PAIR), jnp.bfloat16),
            pltpu.VMEM((4, 8, 128), jnp.float32),
            pltpu.VMEM((8, 128), jnp.float32),
            pltpu.SMEM((2, 2), jnp.int32),
            pltpu.VMEM((2, PAIR, 8 * TOK), jnp.float32),
            pltpu.VMEM((2, 1, 8 * TOK), jnp.float32),
            pltpu.VMEM((8, TOK, PAIR), jnp.bfloat16),
            pltpu.SemaphoreType.DMA,
            pltpu.SemaphoreType.DMA,
            pltpu.SemaphoreType.DMA((len(BATCHES),)),
            pltpu.SemaphoreType.DMA((GROUPS,)),
            pltpu.SemaphoreType.DMA,
            pltpu.SemaphoreType.DMA((GROUPS,)),
            pltpu.SemaphoreType.DMA((3,)),
            pltpu.SemaphoreType.DMA((3,)),
            pltpu.SemaphoreType.DMA,
            pltpu.SemaphoreType.DMA,
            pltpu.SemaphoreType.DMA,
            pltpu.SemaphoreType.REGULAR,
            pltpu.SemaphoreType.REGULAR,
            pltpu.SemaphoreType.REGULAR,
        ],
        compiler_params=pltpu.CompilerParams(
            collective_id=0, has_side_effects=True, vmem_limit_bytes=48 * 1024 * 1024
        ),
    )(queries, bank, read_mask)


def solution(mesh):
    return jax.shard_map(
        body,
        mesh=mesh,
        in_specs=(P("dp", "tok", "frame"), P("dp", "frame", "tok", None), P("dp", "frame")),
        out_specs=P("dp", "tok", "frame"),
        check_vma=False,
    )
```

```python
import math

import jax
import jax.numpy as jnp
from jax import lax
from jax.experimental import pallas as pl
from jax.experimental.pallas import tpu as pltpu
from jax.sharding import PartitionSpec as P

MESH = pl.DeviceIdType.MESH
HEAD_DIM = 64
PAIR = 2 * HEAD_DIM
TOK = 64
KEYS_COLS = 2048
MASKED = -1e30
FLOOR = -1e20

ORDER = (0, 4, 12, 1, 3, 16, 20, 5, 28, 15, 24, 2, 8, 7, 13, 6, 9, 11, 17, 19, 21, 31, 23, 29, 18, 14, 25, 27, 22, 30, 10, 26)
SIZES = (4, 4, 4, 4, 4, 4, 4, 4)
STARTS = tuple(sum(SIZES[:i]) for i in range(len(SIZES)))
GROUPS = len(SIZES)
BATCHES = (6,) + (2,) * 13
BATCH_STARTS = tuple(sum(BATCHES[:i]) for i in range(len(BATCHES)))
GROUP_OF = tuple(i for i, size in enumerate(SIZES) for _ in range(size))
NEAR = 7
FLY = 10


def kernel(q_ref, bank_ref, mask_ref, out_ref, q_buf, q_heads, kv, bias, mask_tile, mask_smem, acc, peak, outs,
           q_send, q_recv, kv_send, kv_recv, fwd_send, fwd_recv, mask_send, mask_recv, mask_copy,
           out_send, out_recv, plane_sem, sibling_sem, far_sem):
    frame, tok = lax.axis_index("frame"), lax.axis_index("tok")
    y, core = frame // 2, frame % 2
    x, z = tok // 4, tok % 4
    samp, pair = tok // 8, tok % 8
    sibling = 2 * y + 1 - core
    across = (frame + 2) % 4
    x_mates = [((x + i) % 4) * 4 + z for i in range(1, 4)]
    z_mates = [x * 4 + (z + i) % 4 for i in range(1, 4)]

    def tell(sem, to_frame, to_tok):
        pl.semaphore_signal(sem, inc=1, device_id={"frame": to_frame, "tok": to_tok}, device_id_type=MESH)

    def send(src, dst, send_sem, recv_sem, to_frame, to_tok):
        copy = pltpu.make_async_remote_copy(
            src, dst, send_sem, recv_sem, device_id={"frame": to_frame, "tok": to_tok}, device_id_type=MESH
        )
        copy.start()

    def send_or_keep(src, dst, send_sem, recv_sem, to_frame, to_tok):
        here = (to_frame == frame) & (to_tok == tok)

        @pl.when(here)
        def _():
            pltpu.make_async_copy(src, dst, recv_sem).start()

        @pl.when(jnp.logical_not(here))
        def _():
            send(src, dst, send_sem, recv_sem, to_frame, to_tok)

    def wait_bytes(ref, sem):
        pltpu.make_async_copy(ref, ref, sem).wait()

    def wait_sent(blocks, sem, kept):
        @pl.when(kept)
        def _():
            wait_bytes(blocks.at[pl.ds(0, 7)], sem)

        @pl.when(jnp.logical_not(kept))
        def _():
            wait_bytes(blocks, sem)

    def send_batch(batch):
        for slot in range(BATCH_STARTS[batch], BATCH_STARTS[batch] + BATCHES[batch]):
            code = ORDER[slot]
            dy, dx, dz = code // 16, code // 4 % 4, code % 4
            dx = jnp.where(core == 1, (4 - dx) % 4, dx)
            dz = jnp.where(core == 1, (4 - dz) % 4, dz)
            to_y, to_tok = (y + dy) % 2, (x + dx) % 4 * 4 + (z + dz) % 4
            column = (8 * to_y + to_tok % 8) * PAIR
            arrived = kv_recv.at[GROUP_OF[slot]]
            for part in range(2):
                src = bank_ref.at[to_tok // 8, :, :, pl.ds(pl.multiple_of(part * KEYS_COLS + column, PAIR), PAIR)]
                dst = kv.at[0, slot, part]
                if code == 0:
                    pltpu.make_async_copy(src, dst, arrived).start()
                else:
                    send(src, dst, kv_send.at[batch], arrived, 2 * to_y + core, to_tok)

    def wait_batch_sent(batch):
        sent = BATCHES[batch] - (1 if batch == 0 else 0)
        wait_bytes(kv.at[0, pl.ds(0, sent)], kv_send.at[batch])

    def send_next(batch):
        if batch < len(BATCHES):
            wait_batch_sent(batch - FLY)
            send_batch(batch)

    barrier = pltpu.get_barrier_semaphore()
    tell(barrier, sibling, tok)
    tell(barrier, across, tok)
    for mate in x_mates + z_mates:
        tell(barrier, frame, mate)
    pltpu.make_async_copy(mask_ref, mask_smem, mask_copy).start()
    mask_tile[...] = jnp.zeros_like(mask_tile)
    acc[...] = jnp.zeros_like(acc)
    peak[...] = jnp.full_like(peak, FLOOR)
    wait_bytes(mask_smem, mask_copy)
    for s in range(2):
        for j in range(2):
            flag = (mask_smem[s, j].astype(jnp.float32) - 1.0) * (-MASKED)
            mask_tile[pl.ds(2 * s + j, 1), :] = jnp.full((1, 128), flag, jnp.float32)
    bias[pl.ds(frame, 1)] = mask_tile[...][None]
    pl.semaphore_wait(barrier, 8)

    for mate in x_mates:
        tell(plane_sem, frame, mate)
    mine_mask, far_mask = bias.at[frame], bias.at[across]
    send(mask_tile, mine_mask, mask_send.at[0], mask_recv.at[0], across, tok)
    send(mask_tile, mine_mask, mask_send.at[1], mask_recv.at[1], sibling, tok)
    send_batch(0)
    pl.semaphore_wait(plane_sem, 3)

    tell(sibling_sem, sibling, tok)
    tell(far_sem, across, tok)
    pl.semaphore_wait(sibling_sem, 1)
    for s in range(2):
        for j in range(4):
            send_or_keep(
                q_ref.at[s, :, pl.ds(j * PAIR, PAIR)], q_buf.at[tok % 8], q_send, q_recv,
                2 * y + tok // 8, 8 * s + 4 * core + j,
            )
    wait_bytes(far_mask, mask_recv.at[0])
    send(far_mask, far_mask, mask_send.at[2], mask_recv.at[2], sibling, tok)
    for batch in range(1, NEAR):
        send_batch(batch)
    pl.semaphore_wait(far_sem, 1)
    for batch in range(NEAR, FLY):
        send_batch(batch)
    send_next(FLY)
    wait_bytes(q_buf, q_recv)
    wait_bytes(mine_mask, mask_recv.at[1])
    wait_bytes(mine_mask, mask_recv.at[2])
    queries = q_buf[...].reshape(8 * TOK, PAIR).astype(jnp.float32) * (1.0 / math.sqrt(HEAD_DIM))
    first = lax.broadcasted_iota(jnp.int32, queries.shape, 1) < HEAD_DIM
    q_heads[0] = jnp.where(first, queries, 0.0).astype(jnp.bfloat16)
    q_heads[1] = jnp.where(first, 0.0, queries).astype(jnp.bfloat16)

    def work(half, group, from_core):
        start, size = STARTS[group], SIZES[group]
        keys = kv[half, pl.ds(start, size), 0].reshape(size * 2 * TOK, PAIR)
        values = kv[half, pl.ds(start, size), 1].reshape(size * 2 * TOK, PAIR)
        values_t = values.T
        top = lax.broadcasted_iota(jnp.int32, values_t.shape, 0) < HEAD_DIM
        one = jnp.ones_like(values_t)
        biases = []
        for i in range(size):
            dy = ORDER[start + i] // 16
            from_frame = 2 * ((y + dy) % 2) + from_core
            for j in range(2):
                row = bias[pl.ds(from_frame, 1), pl.ds(2 * samp + j, 1), :].reshape(1, 128)
                biases.append(jnp.concatenate([row] * 4, axis=1))
        both = [
            lax.dot_general(
                keys, q_heads[head], (((1,), (1,)), ((), ())), preferred_element_type=jnp.float32
            ).reshape(size * 2, TOK, 8 * TOK)
            for head in range(2)
        ]
        for head, scores in enumerate(both):
            old = peak[head]
            new = old
            for i in range(size * 2):
                new = jnp.maximum(new, scores[i].max(axis=0, keepdims=True) + biases[i])
            peak[head] = new
            probs = jnp.concatenate(
                [jnp.exp(scores[i] - (new - biases[i])).astype(jnp.bfloat16) for i in range(size * 2)], axis=0
            )
            weighed = jnp.where(top, values_t, one) if head == 0 else jnp.where(top, one, values_t)
            acc[head] = acc[head] * jnp.exp(old - new) + jnp.dot(weighed, probs, preferred_element_type=jnp.float32)

    def theirs(group):
        return kv.at[1, pl.ds(STARTS[group], SIZES[group])]

    def work_theirs(group):
        wait_bytes(theirs(group), fwd_recv.at[group])
        work(1, group, 1 - core)

    for group in range(GROUPS):
        mine = kv.at[0, pl.ds(STARTS[group], SIZES[group])]
        send_next(FLY + 1 + 2 * group)
        send_next(FLY + 2 + 2 * group)
        if group == GROUPS - 1:
            work_theirs(group - 1)
        wait_bytes(mine, kv_recv.at[group])
        send(mine, theirs(group), fwd_send, fwd_recv.at[group], sibling, tok)
        work(0, group, core)
        if 0 < group < GROUPS - 1:
            work_theirs(group - 1)
    work_theirs(GROUPS - 1)

    result = jnp.concatenate(
        [acc[0, :HEAD_DIM] / acc[0, HEAD_DIM:], acc[1, HEAD_DIM:] / acc[1, :HEAD_DIM]], axis=0
    )
    outs[...] = result.T.astype(jnp.bfloat16).reshape(8, TOK, PAIR)
    owner_frame = 2 * y + pair // 4
    for i in range(8):
        column = pl.multiple_of(pair % 4 * PAIR, PAIR)
        send_or_keep(
            outs.at[i], out_ref.at[samp, :, pl.ds(column, PAIR)], out_send, out_recv, owner_frame, 8 * core + i
        )

    wait_bytes(out_ref, out_recv)
    kept = (tok // 8 == core) & (pair // 4 == core)
    wait_sent(outs, out_send, kept)
    wait_sent(q_buf, q_send, kept)
    for i in range(3):
        wait_bytes(mask_tile, mask_send.at[i])
    for batch in range(len(BATCHES) - FLY, len(BATCHES)):
        wait_batch_sent(batch)
    wait_bytes(kv.at[0], fwd_send)


def body(queries, bank, read_mask):
    return pl.pallas_call(
        kernel,
        out_shape=jax.ShapeDtypeStruct(queries.shape, queries.dtype),
        in_specs=[
            pl.BlockSpec(memory_space=pltpu.HBM),
            pl.BlockSpec(memory_space=pltpu.HBM),
            pl.BlockSpec(memory_space=pltpu.HBM),
        ],
        out_specs=pl.BlockSpec(memory_space=pl.ANY),
        scratch_shapes=[
            pltpu.VMEM((8, TOK, PAIR), jnp.bfloat16),
            pltpu.VMEM((2, 8 * TOK, PAIR), jnp.bfloat16),
            pltpu.VMEM((2, 32, 2, 2, TOK, PAIR), jnp.bfloat16),
            pltpu.VMEM((4, 8, 128), jnp.float32),
            pltpu.VMEM((8, 128), jnp.float32),
            pltpu.SMEM((2, 2), jnp.int32),
            pltpu.VMEM((2, PAIR, 8 * TOK), jnp.float32),
            pltpu.VMEM((2, 1, 8 * TOK), jnp.float32),
            pltpu.VMEM((8, TOK, PAIR), jnp.bfloat16),
            pltpu.SemaphoreType.DMA,
            pltpu.SemaphoreType.DMA,
            pltpu.SemaphoreType.DMA((len(BATCHES),)),
            pltpu.SemaphoreType.DMA((GROUPS,)),
            pltpu.SemaphoreType.DMA,
            pltpu.SemaphoreType.DMA((GROUPS,)),
            pltpu.SemaphoreType.DMA((3,)),
            pltpu.SemaphoreType.DMA((3,)),
            pltpu.SemaphoreType.DMA,
            pltpu.SemaphoreType.DMA,
            pltpu.SemaphoreType.DMA,
            pltpu.SemaphoreType.REGULAR,
            pltpu.SemaphoreType.REGULAR,
            pltpu.SemaphoreType.REGULAR,
        ],
        compiler_params=pltpu.CompilerParams(
            collective_id=0, has_side_effects=True, vmem_limit_bytes=48 * 1024 * 1024
        ),
    )(queries, bank, read_mask)


def solution(mesh):
    return jax.shard_map(
        body,
        mesh=mesh,
        in_specs=(P("dp", "tok", "frame"), P("dp", "frame", "tok", None), P("dp", "frame")),
        out_specs=P("dp", "tok", "frame"),
        check_vma=False,
    )
```
